128 devices in a mesh: dp: 128 (over y, z, x, core).
Axes of the slice: x: 4, y: 4, z: 4, core: 2. Of those that a mesh axis runs over, the one named last changes fastest.
Arguments:
- clips: bfloat16 [131072, 1152], P('dp'), may hold values from -0.1875 to 0.1875
- captions: bfloat16 [131072, 1152], P('dp'), may hold values from -0.1875 to 0.1875
- positive: int32 [131072], P('dp'), may hold values from 0 to 131071, as said below
- log_scale: float32 [1], replicated, may hold values from 1.6 to 2.6
- bias: float32 [1], replicated, may hold values from -3 to -1
Outputs:
- clip_grad: bfloat16 [131072, 1152], P('dp')
- caption_grad: bfloat16 [131072, 1152], P('dp')
The draws below stay inside these ranges and needn't reach their ends.
Inputs may be any that keep to these rules, and one draw needn't show every extreme that they name: For a clip row of block k, positive names a caption row of one of the blocks (k - s) mod (131072 / 1024) with 0 <= s < 4.
All inputs are finite; a program needn't handle non-finite values.
Results may differ from the reference program's by a relative error of at most 0.0048.
Values may be sent and summed in bfloat16 or wider, within the bound.
No kernel may reach another device: no remote copies, remote signals or barrier semaphores. Data moves between devices by JAX's collectives and lax.ppermute only.
A program may use at most 128 MiB of HBM per device.

```python
import jax
import jax.numpy as jnp
from jax import lax

D = 1152
ROWS = 1024
STEPS = 4
CAPTIONS = 131072


def draw_positive(key, part):
    key = jax.random.fold_in(key, 5)
    key_step, key_row = jax.random.split(key)
    blocks = CAPTIONS // ROWS
    index = jnp.arange(CAPTIONS, dtype=jnp.int32)
    owner = index // ROWS
    offset = jax.random.randint(key_step, (CAPTIONS,), 0, STEPS, dtype=jnp.int32)
    within = jax.random.randint(key_row, (CAPTIONS,), 0, ROWS, dtype=jnp.int32)
    edge_low = index == 0
    edge_high = index == CAPTIONS - 1
    offset = jnp.where(edge_low | edge_high, 0, offset)
    within = jnp.where(edge_low, 0, jnp.where(edge_high, ROWS - 1, within))
    return ((owner - offset) % blocks * ROWS + within).astype(jnp.int32)


def shard_levels(rng, extent, pieces, smallest, top_value):
    gain, own = 1.0, jax.random.fold_in(rng, 6)
    for position, shards_of in pieces:
        steps = jnp.exp(jax.random.uniform(jax.random.fold_in(own, position), (shards_of,), jnp.float32, smallest / len(pieces), top_value / len(pieces)))
        gain = gain * jnp.repeat(steps, extent[position] // shards_of).reshape([-1 if axis == position else 1 for axis in range(len(extent))])
    return gain


def noise(own_key, dims, scale, reach, cuts=(), held_as=jnp.bfloat16):
    values = jax.random.normal(own_key, dims, jnp.float32) * scale
    if len(cuts) > 0:
        values = shard_levels(own_key, dims, cuts, -0.22, 0.18) * values
    return jnp.clip(values, min=-reach, max=reach).astype(held_as)


def setup_inputs(seed: int = 0) -> dict:
    splits = jax.random.split(jax.random.key(seed), 6)
    return {
        "clips": noise(splits[0], (CAPTIONS, D), D ** -0.5, 0.1875, ((0, 128),)),
        "captions": noise(splits[1], (CAPTIONS, D), D ** -0.5, 0.1875, ((0, 128),)),
        "positive": draw_positive(jax.random.fold_in(splits[5], 71), 0),
        "log_scale": jnp.clip(jax.random.uniform(splits[3], (1,), jnp.float32, 1.6, 2.6), 1.6, 2.6),
        "bias": jnp.clip(jax.random.uniform(splits[4], (1,), jnp.float32, -3.0, -1.0), -3.0, -1.0),
    }


def reference(clips, captions, positive, log_scale, bias):
    blocks = CAPTIONS // ROWS
    scale = jnp.exp(log_scale[0])
    shift = bias[0]
    column = jnp.arange(ROWS, dtype=jnp.int32)

    def per_block(carry, index):
        start = (index * ROWS).astype(jnp.int32)
        clip_rows = lax.dynamic_slice_in_dim(clips, start, ROWS, 0)
        pos_rows = lax.dynamic_slice_in_dim(positive, start, ROWS, 0)
        clip_sum = jnp.zeros((ROWS, D), jnp.float32)
        for offset in range(STEPS):
            owner = ((index - offset) % blocks).astype(jnp.int32)
            first = (owner * ROWS).astype(jnp.int32)
            cap_rows = lax.dynamic_slice_in_dim(captions, first, ROWS, 0)
            logit = scale * lax.dot_general(clip_rows, cap_rows, (((1,), (1,)), ((), ())), preferred_element_type=jnp.float32) + shift
            label = jnp.where(pos_rows[:, None] == first + column[None, :], 1.0, -1.0).astype(jnp.float32)
            coef = (scale * (-label * jax.nn.sigmoid(-label * logit))).astype(jnp.bfloat16)
            clip_sum = clip_sum + jnp.dot(coef, cap_rows, preferred_element_type=jnp.float32)
            term = lax.dot_general(coef, clip_rows, (((0,), (0,)), ((), ())), preferred_element_type=jnp.float32)
            old = lax.dynamic_slice_in_dim(carry, first, ROWS, 0)
            carry = lax.dynamic_update_slice_in_dim(carry, old + term, first, 0)
        return carry, clip_sum.astype(jnp.bfloat16)

    start_sum = jnp.zeros((CAPTIONS, D), jnp.float32)
    caption_sum, clip_parts = lax.scan(per_block, start_sum, jnp.arange(blocks, dtype=jnp.int32))
    clip_grad = clip_parts.reshape(CAPTIONS, D)
    return clip_grad, caption_sum.astype(jnp.bfloat16)
```

```python
import functools

import jax
import jax.numpy as jnp
from jax import lax
from jax.experimental import pallas as pl
from jax.experimental.pallas import tpu as pltpu
from jax.sharding import PartitionSpec as P

TILE = 256
CHUNK = 256


def band_kernel(pairs, has_sum, scalars, rows, row_ids, *refs):
    cols = refs[: 2 * pairs]
    rest = refs[2 * pairs :]
    out = rest[-1]
    scale = scalars[0]
    shift = scalars[1]
    block = rows[...]
    ids = row_ids[...]
    total = rest[0][...] if has_sum else None
    work = []
    for p in range(pairs):
        height = cols[2 * p].shape[0]
        for j in range(height // CHUNK):
            work.append((cols[2 * p], cols[2 * p + 1], j * CHUNK))

    def logits(item):
        col, _, start = item
        return lax.dot_general(
            block,
            col[start : start + CHUNK, :],
            (((1,), (1,)), ((), ())),
            preferred_element_type=jnp.float32,
        )

    ahead = logits(work[0])
    for n, item in enumerate(work):
        now = ahead
        if n + 1 < len(work):
            ahead = logits(work[n + 1])
        col, col_ids, start = item
        hit = ids == col_ids[:, start : start + CHUNK]
        z = scale * now + shift
        share = 1.0 / (1.0 + jnp.exp(jnp.where(hit, z, -z)))
        coef = (jnp.where(hit, -scale, scale) * share).astype(jnp.bfloat16)
        term = jnp.dot(coef, col[start : start + CHUNK, :], preferred_element_type=jnp.float32)
        total = term if total is None else total + term
    out[...] = total.astype(out.dtype)


def band(scalars, rows, row_ids, cols, summed=None, dtype=jnp.float32):
    height, width = rows.shape
    pairs = len(cols)
    whole = lambda i: (0, 0)
    tile = lambda i: (i, 0)
    in_specs = [
        pl.BlockSpec(memory_space=pltpu.SMEM),
        pl.BlockSpec((TILE, width), tile),
        pl.BlockSpec((TILE, 1), tile),
    ]
    args = [scalars, rows, row_ids[:, None]]
    for col, col_ids in cols:
        in_specs += [pl.BlockSpec(col.shape, whole), pl.BlockSpec((1, col.shape[0]), whole)]
        args += [col, col_ids[None, :]]
    if summed is not None:
        in_specs.append(pl.BlockSpec((TILE, width), tile))
        args.append(summed)
    flops = 4 * pairs * height * height * width
    return pl.pallas_call(
        functools.partial(band_kernel, pairs, summed is not None),
        grid=(height // TILE,),
        out_shape=jax.ShapeDtypeStruct((height, width), dtype),
        in_specs=in_specs,
        out_specs=pl.BlockSpec((TILE, width), tile),
        compiler_params=pltpu.CompilerParams(vmem_limit_bytes=48 * 1024 * 1024),
        cost_estimate=pl.CostEstimate(
            flops=flops, bytes_accessed=8 * height * width, transcendentals=pairs * height * height
        ),
    )(*args)


def shards(clips, captions, positive, log_scale, bias):
    rows = clips.shape[0]
    count = lax.axis_size("dp")
    mine = lax.axis_index("dp")
    even = mine % 2 == 0
    scalars = jnp.concatenate([jnp.exp(log_scale), bias])
    evens = range(0, count, 2)
    odds = range(1, count, 2)

    def move(value, pairs):
        return lax.ppermute(value, "dp", [(i, j % count) for i, j in pairs])

    def swap(value):
        return move(value, [(i, i ^ 1) for i in range(count)])

    apart = [(i, i - 2) for i in evens] + [(i, i + 2) for i in odds]
    together = [(i, i + 2) for i in evens] + [(i, i - 2) for i in odds]

    def caption_ids(owner):
        return (owner % count) * rows + jnp.arange(rows, dtype=jnp.int32)

    next_clip = move(clips, [(i, i - 2) for i in evens])
    last_caption = move(captions, [(i, i + 2) for i in odds])

    next_pos = move(positive, [(i, i - 2) for i in range(count)])
    other_pos = swap(jnp.stack([positive, next_pos]))
    x_ids = jnp.where(even, caption_ids(mine), positive)
    y_ids = jnp.where(even, positive, caption_ids(mine))
    w_ids = jnp.where(even, other_pos[0], caption_ids(mine - 1))
    u1_ids = jnp.where(even, next_pos, caption_ids(mine - 2))
    v1_ids = jnp.where(even, caption_ids(mine - 1), other_pos[1])
    u2_ids = jnp.where(even, other_pos[1], caption_ids(mine - 3))
    v2_ids = jnp.where(even, caption_ids(mine - 2), next_pos)

    x = jnp.where(even, captions, clips)
    y = jnp.where(even, clips, captions)
    w = swap(x)
    gy = band(scalars, y, y_ids, [(x, x_ids)])
    gx = band(scalars, x, x_ids, [(y, y_ids), (w, w_ids)])

    v2 = move(x, together)

    u1 = jnp.where(even, next_clip, last_caption)
    v1 = swap(u1)
    gu = band(scalars, u1, u1_ids, [(v1, v1_ids)], dtype=jnp.bfloat16)
    back = move(gu, together)
    gx = band(scalars, x, x_ids, [(u1, u1_ids)], gx)
    gy = band(scalars, y, y_ids, [(v1, v1_ids)], gy)

    u2 = swap(v2)
    gy = band(scalars, y, y_ids, [(v2, v2_ids)], gy)
    gx = band(scalars, x, x_ids, [(u2, u2_ids)], gx, dtype=jnp.bfloat16)
    gy = (gy + back.astype(jnp.float32)).astype(jnp.bfloat16)
    return jnp.where(even, gy, gx), jnp.where(even, gx, gy)


def solution(mesh):
    in_specs = (P("dp", None), P("dp", None), P("dp"), P(), P())
    out_specs = (P("dp", None), P("dp", None))
    return jax.shard_map(shards, mesh=mesh, in_specs=in_specs, out_specs=out_specs, check_vma=False)
```

```python
import functools

import jax
import jax.numpy as jnp
from jax import lax
from jax.experimental import pallas as pl
from jax.experimental.pallas import tpu as pltpu
from jax.sharding import PartitionSpec as P

TILE = 512
PART = 256
LOG2_E = 1.4426950408889634


def band_kernel(pairs, has_sum, passes, scalars, rows, row_ids, *refs):
    cols = refs[: 2 * pairs]
    rest = refs[2 * pairs :]
    summed = rest[0] if has_sum else None
    out = rest[1] if has_sum else rest[0]
    scale = scalars[0]
    slope = -LOG2_E * scale
    start = -LOG2_E * scalars[1]
    work = [(r, p) for r in range(0, rows.shape[0], PART) for p in range(pairs)]

    def logits(item):
        r, p = item
        return lax.dot_general(
            rows[r : r + PART, :],
            cols[2 * p][...],
            (((1,), (1,)), ((), ())),
            preferred_element_type=jnp.float32,
        )

    ahead = logits(work[0])
    total = None
    for n, (r, p) in enumerate(work):
        now = ahead
        if n + 1 < len(work):
            ahead = logits(work[n + 1])
        hit = row_ids[r : r + PART, :] == cols[2 * p + 1][...]
        power = slope * now + start
        share = pl.reciprocal(1.0 + jnp.exp2(jnp.where(hit, -power, power)), approx=True)
        coef = (jnp.where(hit, -scale, scale) * share).astype(jnp.bfloat16)
        term = jnp.dot(coef, cols[2 * p][...], preferred_element_type=jnp.float32)
        if p == 0:
            total = summed[r : r + PART, :] + term if has_sum else term
        else:
            total = total + term
        if p == pairs - 1:
            out[r : r + PART, :] = total.astype(out.dtype)
    if passes:
        rest[-1][...] = rows[...]


def band(scalars, rows, row_ids, cols, summed=None, dtype=jnp.float32, passes=False):
    height, width = rows.shape
    pairs = len(cols)
    whole = lambda i: (0, 0)
    tile = lambda i: (i, 0)
    in_specs = [
        pl.BlockSpec(memory_space=pltpu.SMEM),
        pl.BlockSpec((TILE, width), tile),
        pl.BlockSpec((TILE, 1), tile),
    ]
    args = [scalars, rows, row_ids[:, None]]
    for col, col_ids in cols:
        in_specs += [pl.BlockSpec(col.shape, whole), pl.BlockSpec((1, col.shape[0]), whole)]
        args += [col, col_ids[None, :]]
    if summed is not None:
        in_specs.append(pl.BlockSpec((TILE, width), tile))
        args.append(summed)
    out_shape = [jax.ShapeDtypeStruct((height, width), dtype)]
    if passes:
        out_shape.append(jax.ShapeDtypeStruct((height, width), rows.dtype))
    flops = 4 * pairs * height * height * width
    results = pl.pallas_call(
        functools.partial(band_kernel, pairs, summed is not None, passes),
        grid=(height // TILE,),
        out_shape=out_shape,
        in_specs=in_specs,
        out_specs=[pl.BlockSpec((TILE, width), tile)] * len(out_shape),
        compiler_params=pltpu.CompilerParams(vmem_limit_bytes=40 * 1024 * 1024),
        cost_estimate=pl.CostEstimate(
            flops=flops, bytes_accessed=8 * height * width, transcendentals=pairs * height * height
        ),
    )(*args)
    return results if passes else results[0]


def shards(clips, captions, positive, log_scale, bias):
    rows = clips.shape[0]
    count = lax.axis_size("dp")
    mine = lax.axis_index("dp")
    even = mine % 2 == 0
    scalars = jnp.concatenate([jnp.exp(log_scale), bias])
    evens = range(0, count, 2)
    odds = range(1, count, 2)

    def move(value, pairs):
        return lax.ppermute(value, "dp", [(i, j % count) for i, j in pairs])

    def swap(value):
        return move(value, [(i, i ^ 1) for i in range(count)])

    apart = [(i, i - 2) for i in evens] + [(i, i + 2) for i in odds]
    home = [(i, i - 1) for i in evens] + [(i, i + 1) for i in odds]

    def caption_ids(owner):
        return (owner % count) * rows + jnp.arange(rows, dtype=jnp.int32)

    y = jnp.where(even, clips, captions)
    u1 = move(y, apart)
    y, clips, captions = lax.optimization_barrier((y, clips, captions))
    x = jnp.where(even, captions, clips)
    w = swap(x)
    u2 = move(w, apart)

    other_pos = swap(positive)
    chip_pos = jnp.stack([other_pos, positive])
    next_pos = jnp.where(
        even, move(chip_pos, [(i, i - 3) for i in odds]), move(chip_pos, [(i, i - 2) for i in odds])
    )
    x_ids = jnp.where(even, caption_ids(mine), positive)
    y_ids = jnp.where(even, positive, caption_ids(mine))
    w_ids = jnp.where(even, other_pos, caption_ids(mine - 1))
    u1_ids = jnp.where(even, next_pos[0], caption_ids(mine - 2))
    v1_ids = jnp.where(even, caption_ids(mine - 1), next_pos[0])
    u2_ids = jnp.where(even, next_pos[1], caption_ids(mine - 3))
    v2_ids = jnp.where(even, caption_ids(mine - 2), next_pos[1])

    gx = band(scalars, x, x_ids, [(y, y_ids)])
    gy = band(scalars, y, y_ids, [(x, x_ids)])
    gx = band(scalars, x, x_ids, [(w, w_ids)], gx)

    u1, gx, gy = lax.optimization_barrier((u1, gx, gy))
    v1 = swap(u1)
    gv = band(scalars, v1, v1_ids, [(u1, u1_ids)], dtype=jnp.bfloat16)
    back = move(gv, home)
    u1, v1, gv = lax.optimization_barrier((u1, v1, gv))
    gx = band(scalars, x, x_ids, [(u1, u1_ids)], gx)
    gy = band(scalars, y, y_ids, [(v1, v1_ids)], gy)

    u2, gx = lax.optimization_barrier((u2, gx))
    v2 = swap(u2)
    gx = band(scalars, x, x_ids, [(u2, u2_ids)], gx, dtype=jnp.bfloat16)
    gy = band(scalars, y, y_ids, [(v2, v2_ids)], gy)
    back, gx, gy = lax.optimization_barrier((back, gx, gy))
    gy = (gy + back.astype(jnp.float32)).astype(jnp.bfloat16)
    return jnp.where(even, gy, gx), jnp.where(even, gx, gy)


def solution(mesh):
    in_specs = (P("dp", None), P("dp", None), P("dp"), P(), P())
    out_specs = (P("dp", None), P("dp", None))
    return jax.shard_map(shards, mesh=mesh, in_specs=in_specs, out_specs=out_specs, check_vma=False)
```

```python
import functools

import jax
import jax.numpy as jnp
from jax import lax
from jax.experimental import pallas as pl
from jax.experimental.pallas import tpu as pltpu
from jax.sharding import PartitionSpec as P

PART = 256
LOG2_E = 1.4426950408889634
SMEM_SPEC = pl.BlockSpec(memory_space=pltpu.SMEM)
VMEM_SPEC = pl.BlockSpec(memory_space=pltpu.VMEM)
ANY_SPEC = pl.BlockSpec(memory_space=pl.ANY)
COST = pl.CostEstimate(flops=1, bytes_accessed=1, transcendentals=0)
PARAMS = pltpu.CompilerParams(vmem_limit_bytes=20 * 1024 * 1024)


def upright(ids):
    return jnp.transpose(jnp.broadcast_to(ids, (128, ids.shape[1])))[:, :1]


def accumulate(scalars, groups):
    scale = scalars[0]
    slope = -LOG2_E * scale
    start = -LOG2_E * scalars[1]
    work = [
        (g, r, p)
        for g in range(len(groups))
        for r in range(0, groups[g][0].shape[0], PART)
        for p in range(len(groups[g][2]))
    ]

    def logits(item):
        g, r, p = item
        rows, _, cols, _, _ = groups[g]
        return lax.dot_general(
            rows[r : r + PART, :],
            cols[p][0][...],
            (((1,), (1,)), ((), ())),
            preferred_element_type=jnp.float32,
        )

    ahead = logits(work[0])
    total = None
    for n, (g, r, p) in enumerate(work):
        _, row_ids, cols, summed, store = groups[g]
        now = ahead
        if n + 1 < len(work):
            ahead = logits(work[n + 1])
        hit = upright(row_ids[:, r : r + PART]) == cols[p][1][...]
        power = slope * now + start
        share = pl.reciprocal(1.0 + jnp.exp2(jnp.where(hit, -power, power)), approx=True)
        coef = (jnp.where(hit, -scale, scale) * share).astype(jnp.bfloat16)
        term = jnp.dot(coef, cols[p][0][...], preferred_element_type=jnp.float32)
        if p == 0:
            total = term if summed is None else summed[r : r + PART, :] + term
        else:
            total = total + term
        if p == len(cols) - 1:
            store(r, total)


def store_to(ref, base=0):
    def store(r, value):
        ref[base + r : base + r + PART, :] = value.astype(ref.dtype)

    return store


def unpack(shape, refs):
    groups = []
    for pairs, has_sum in shape:
        rows, row_ids = refs.pop(0), refs.pop(0)
        cols = [(refs.pop(0), refs.pop(0)) for _ in range(pairs)]
        groups.append((rows, row_ids, cols, refs.pop(0) if has_sum else None))
    return groups


def flatten(groups, first):
    shape, args, sums = [], [], []
    for rows, row_ids, cols, summed in groups:
        args += [rows, row_ids[None, :]]
        for col, col_ids in cols:
            args += [col, col_ids[None, :]]
        if summed is not None:
            sums.append(first + len(args))
            args.append(summed)
        shape.append((len(cols), summed is not None))
    return shape, args, sums


def band_kernel(shape, places, carried, scalars, _, *refs):
    refs = list(refs)
    groups = unpack(shape, refs)
    outs = refs[carried:]
    accumulate(scalars, [group + (store_to(outs[n], base),) for group, (n, base) in zip(groups, places)])
    refs[-1][...] = jnp.zeros_like(refs[-1])


def band(scalars, token, groups, places, height, dtype=jnp.float32, carried=()):
    width = groups[0][0].shape[1]
    shape, args, sums = flatten(groups, 2)
    outs = 1 + max(n for n, _ in places)
    aliases = {place: n for n, place in enumerate(dict.fromkeys(sums))}
    aliases |= {2 + len(args) + n: outs + n for n in range(len(carried))}
    return pl.pallas_call(
        functools.partial(band_kernel, shape, places, len(carried)),
        out_shape=[pltpu.VMEM((height, width), dtype)] * outs
        + [pltpu.VMEM(value.shape, value.dtype) for value in carried]
        + [jax.ShapeDtypeStruct((8, 128), jnp.float32)],
        in_specs=[SMEM_SPEC, ANY_SPEC] + [VMEM_SPEC] * (len(args) + len(carried)),
        out_specs=[VMEM_SPEC] * (outs + len(carried) + 1),
        input_output_aliases=aliases,
        compiler_params=PARAMS,
        cost_estimate=COST,
    )(scalars, token, *args, *carried)


def after(value, token):
    return lax.optimization_barrier((value, token))


def put(parity, even_target, odd_target, held, r, sem):
    rows = slice(r, r + PART)
    to_even = pltpu.make_async_copy(held.at[rows], even_target.at[rows], sem.at[r // PART])
    to_odd = pltpu.make_async_copy(held.at[rows], odd_target.at[rows], sem.at[r // PART])
    pl.when(parity == 0)(to_even.start)
    pl.when(parity != 0)(to_odd.start)
    return to_even.wait


def last_kernel(shape, scalars, _, parity, *refs):
    refs = list(refs)
    groups = unpack(shape, refs)
    gy0, gy1, clip_grad, caption_grad, held, sem = refs
    waits = []

    def store(base):
        def inner(r, value):
            held[base + r : base + r + PART, :] = value.astype(held.dtype)
            waits.append(put(parity[0], caption_grad, clip_grad, held, base + r, sem))

        return inner

    stores = [store(0), store(groups[0][0].shape[0]), store_to(gy0), store_to(gy1)]
    accumulate(scalars, [group + (one,) for group, one in zip(groups, stores)])
    for wait in waits:
        wait()


def last_pair(scalars, token, parity, groups, dtype):
    half, width = groups[0][0].shape
    shape, args, sums = flatten(groups, 3)
    grad = jax.ShapeDtypeStruct((2 * half, width), dtype)
    return pl.pallas_call(
        functools.partial(last_kernel, shape),
        out_shape=[pltpu.VMEM((half, width), jnp.float32)] * 2 + [grad, grad],
        in_specs=[SMEM_SPEC, ANY_SPEC, SMEM_SPEC] + [VMEM_SPEC] * len(args),
        out_specs=[VMEM_SPEC] * 2 + [ANY_SPEC] * 2,
        scratch_shapes=[pltpu.VMEM((2 * half, width), dtype), pltpu.SemaphoreType.DMA((2 * half // PART,))],
        input_output_aliases={sums[2]: 0, sums[3]: 1},
        compiler_params=PARAMS,
        cost_estimate=COST,
    )(scalars, token, parity, *args)


def close_kernel(parity, gy0, gy1, back, _, __, clip_grad, caption_grad, held, sem):
    half = gy0.shape[0]
    waits = []
    for r in range(0, 2 * half, PART):
        rows = slice(r, r + PART)
        part = (gy0 if r < half else gy1)[r % half : r % half + PART, :]
        held[rows, :] = (part + back[rows, :].astype(jnp.float32)).astype(held.dtype)
        waits.append(put(parity[0], clip_grad, caption_grad, held, r, sem))
    for wait in waits:
        wait()


def close(parity, gy0, gy1, back, clip_grad, caption_grad):
    grad = jax.ShapeDtypeStruct(back.shape, back.dtype)
    return pl.pallas_call(
        close_kernel,
        out_shape=[grad, grad],
        in_specs=[SMEM_SPEC] + [VMEM_SPEC] * 3 + [ANY_SPEC, ANY_SPEC],
        out_specs=[ANY_SPEC, ANY_SPEC],
        scratch_shapes=[pltpu.VMEM(back.shape, back.dtype), pltpu.SemaphoreType.DMA((back.shape[0] // PART,))],
        input_output_aliases={4: 0, 5: 1},
        compiler_params=PARAMS,
        cost_estimate=COST,
    )(parity, gy0, gy1, back, clip_grad, caption_grad)


def shards(clips, captions, positive, log_scale, bias):
    rows = clips.shape[0]
    count = lax.axis_size("dp")
    mine = lax.axis_index("dp")
    even = mine % 2 == 0
    parity = (mine % 2).astype(jnp.int32)[None]
    scalars = jnp.concatenate([jnp.exp(log_scale), bias])
    evens = range(0, count, 2)
    odds = range(1, count, 2)

    def move(value, pairs):
        return lax.ppermute(value, "dp", [(i, j % count) for i, j in pairs])

    def swap(value):
        return move(value, [(i, i ^ 1) for i in range(count)])

    apart = [(i, i - 2) for i in evens] + [(i, i + 2) for i in odds]
    home = [(i, i - 1) for i in evens] + [(i, i + 1) for i in odds]

    def caption_ids(owner):
        return (owner % count) * rows + jnp.arange(rows, dtype=jnp.int32)

    half = rows // 2

    def halves(value):
        return [value[:half], value[half:]]

    def pick(first, second):
        return [jnp.where(even, a, b) for a, b in zip(halves(first), halves(second))]

    def each(step, block):
        return [step(part) for part in block]

    y = pick(clips, captions)
    u1 = each(lambda part: move(part, apart), y)
    y, clips, captions = lax.optimization_barrier((y, clips, captions))
    x = pick(captions, clips)
    w = each(swap, x)

    other_pos = swap(positive)
    chip_pos = jnp.stack([other_pos, positive])
    next_even = move(chip_pos, [(i, i - 3) for i in odds])
    next_odd = move(chip_pos, [(i, i - 2) for i in odds])
    w, next_even, next_odd = lax.optimization_barrier((w, next_even, next_odd))
    u2 = each(lambda part: move(part, apart), w)
    next_pos = jnp.where(even, next_even, next_odd)

    x_ids = halves(jnp.where(even, caption_ids(mine), positive))
    y_ids = halves(jnp.where(even, positive, caption_ids(mine)))
    w_ids = halves(jnp.where(even, other_pos, caption_ids(mine - 1)))
    u1_ids = halves(jnp.where(even, next_pos[0], caption_ids(mine - 2)))
    v1_ids = halves(jnp.where(even, caption_ids(mine - 1), next_pos[0]))
    u2_ids = halves(jnp.where(even, next_pos[1], caption_ids(mine - 3)))
    v2_ids = halves(jnp.where(even, caption_ids(mine - 2), next_pos[1]))
    scalars, u1_ids, v1_ids, u2_ids, v2_ids = lax.optimization_barrier((scalars, u1_ids, v1_ids, u2_ids, v2_ids))

    def group(block, ids, cols, sums=(None, None)):
        pairs = [pair for col, col_ids in cols for pair in zip(col, col_ids)]
        return [(part, part_ids, pairs, total) for part, part_ids, total in zip(block, ids, sums)]

    gx0, gx1, gy0, gy1, token = band(
        scalars,
        jnp.zeros((8, 128), jnp.float32),
        group(x, x_ids, [(y, y_ids), (w, w_ids)]) + group(y, y_ids, [(x, x_ids)]),
        [(0, 0), (1, 0), (2, 0), (3, 0)],
        half,
    )

    u1, token = after(u1, token)
    v1 = each(swap, u1)
    gv, gx0, gx1, gy0, gy1, token = band(
        scalars,
        token,
        group(v1, v1_ids, [(u1, u1_ids)]),
        [(0, 0), (0, half)],
        rows,
        clips.dtype,
        (gx0, gx1, gy0, gy1),
    )
    back = move(gv, home)
    gx0, gx1, gy0, gy1, token = band(
        scalars, token, group(x, x_ids, [(u1, u1_ids)], (gx0, gx1)), [(0, 0), (1, 0)], half, carried=(gy0, gy1)
    )
    u2, token = after(u2, token)
    v2 = each(swap, u2)
    gy0, gy1, gx0, gx1, token = band(
        scalars, token, group(y, y_ids, [(v1, v1_ids)], (gy0, gy1)), [(0, 0), (1, 0)], half, carried=(gx0, gx1)
    )
    gy0, gy1, clip_grad, caption_grad = last_pair(
        scalars,
        token,
        parity,
        group(x, x_ids, [(u2, u2_ids)], (gx0, gx1)) + group(y, y_ids, [(v2, v2_ids)], (gy0, gy1)),
        clips.dtype,
    )
    return tuple(close(parity, gy0, gy1, back, clip_grad, caption_grad))


def solution(mesh):
    in_specs = (P("dp", None), P("dp", None), P("dp"), P(), P())
    out_specs = (P("dp", None), P("dp", None))
    return jax.shard_map(shards, mesh=mesh, in_specs=in_specs, out_specs=out_specs, check_vma=False)
```

```python
import functools

import jax
import jax.numpy as jnp
from jax import lax
from jax.experimental import pallas as pl
from jax.experimental.pallas import tpu as pltpu
from jax.sharding import PartitionSpec as P

PART = 256
LOG2_E = 1.4426950408889634
SMEM_SPEC = pl.BlockSpec(memory_space=pltpu.SMEM)
VMEM_SPEC = pl.BlockSpec(memory_space=pltpu.VMEM)
ANY_SPEC = pl.BlockSpec(memory_space=pl.ANY)
COST = pl.CostEstimate(flops=1, bytes_accessed=1, transcendentals=0)
PARAMS = pltpu.CompilerParams(vmem_limit_bytes=20 * 1024 * 1024)


def upright(ids):
    return jnp.transpose(jnp.broadcast_to(ids, (128, ids.shape[1])))[:, :1]


def accumulate(scalars, groups):
    scale = scalars[0]
    slope = -LOG2_E * scale
    start = -LOG2_E * scalars[1]
    work = [
        (g, r, p)
        for g in range(len(groups))
        for r in range(0, groups[g][0].shape[0], PART)
        for p in range(len(groups[g][2]))
    ]

    def logits(item):
        g, r, p = item
        rows, _, cols, _, _ = groups[g]
        return lax.dot_general(
            rows[r : r + PART, :],
            cols[p][0][...],
            (((1,), (1,)), ((), ())),
            preferred_element_type=jnp.float32,
        )

    ahead = logits(work[0])
    total = None
    for n, (g, r, p) in enumerate(work):
        _, row_ids, cols, summed, store = groups[g]
        now = ahead
        if n + 1 < len(work):
            ahead = logits(work[n + 1])
        hit = upright(row_ids[:, r : r + PART]) == cols[p][1][...]
        power = slope * now + start
        share = pl.reciprocal(1.0 + jnp.exp2(jnp.where(hit, -power, power)), approx=True)
        coef = (jnp.where(hit, -scale, scale) * share).astype(jnp.bfloat16)
        term = jnp.dot(coef, cols[p][0][...], preferred_element_type=jnp.float32)
        if p == 0:
            total = term if summed is None else summed[r : r + PART, :] + term
        else:
            total = total + term
        if p == len(cols) - 1:
            store(r, total)


def store_to(ref, base=0):
    def store(r, value):
        ref[base + r : base + r + PART, :] = value.astype(ref.dtype)

    return store


def unpack(shape, refs):
    groups = []
    for pairs, has_sum in shape:
        rows, row_ids = refs.pop(0), refs.pop(0)
        cols = [(refs.pop(0), refs.pop(0)) for _ in range(pairs)]
        groups.append((rows, row_ids, cols, refs.pop(0) if has_sum else None))
    return groups


def flatten(groups, first):
    shape, args, sums = [], [], []
    for rows, row_ids, cols, summed in groups:
        args += [rows, row_ids[None, :]]
        for col, col_ids in cols:
            args += [col, col_ids[None, :]]
        if summed is not None:
            sums.append(first + len(args))
            args.append(summed)
        shape.append((len(cols), summed is not None))
    return shape, args, sums


def band_kernel(shape, places, carried, scalars, _, *refs):
    refs = list(refs)
    groups = unpack(shape, refs)
    outs = refs[carried:]
    accumulate(scalars, [group + (store_to(outs[n], base),) for group, (n, base) in zip(groups, places)])
    refs[-1][...] = jnp.zeros_like(refs[-1])


def band(scalars, token, groups, places, heights, dtype=jnp.float32, carried=()):
    width = groups[0][0].shape[1]
    shape, args, sums = flatten(groups, 2)
    outs = len(heights)
    aliases = {place: n for n, place in enumerate(dict.fromkeys(sums))}
    aliases |= {2 + len(args) + n: outs + n for n in range(len(carried))}
    return pl.pallas_call(
        functools.partial(band_kernel, shape, places, len(carried)),
        out_shape=[pltpu.VMEM((height, width), dtype) for height in heights]
        + [pltpu.VMEM(value.shape, value.dtype) for value in carried]
        + [jax.ShapeDtypeStruct((8, 128), jnp.float32)],
        in_specs=[SMEM_SPEC, ANY_SPEC] + [VMEM_SPEC] * (len(args) + len(carried)),
        out_specs=[VMEM_SPEC] * (outs + len(carried) + 1),
        input_output_aliases=aliases,
        compiler_params=PARAMS,
        cost_estimate=COST,
    )(scalars, token, *args, *carried)


def after(value, token):
    return lax.optimization_barrier((value, token))


def put(parity, even_target, odd_target, held, r, sem):
    rows = slice(r, r + PART)
    to_even = pltpu.make_async_copy(held.at[rows], even_target.at[rows], sem.at[r // PART])
    to_odd = pltpu.make_async_copy(held.at[rows], odd_target.at[rows], sem.at[r // PART])
    pl.when(parity == 0)(to_even.start)
    pl.when(parity != 0)(to_odd.start)
    return to_even.wait


def last_kernel(shape, scalars, _, parity, *refs):
    refs = list(refs)
    groups = unpack(shape, refs)
    gy0, gy1, clip_grad, caption_grad, held, sem = refs
    waits = []

    def store(r, value):
        held[r : r + PART, :] = value.astype(held.dtype)
        waits.append(put(parity[0], caption_grad, clip_grad, held, r, sem))

    stores = [store, store_to(gy0), store_to(gy1)]
    accumulate(scalars, [group + (one,) for group, one in zip(groups, stores)])
    for wait in waits:
        wait()


def last_pair(scalars, token, parity, groups, dtype):
    rows, width = groups[0][0].shape
    half = rows // 2
    shape, args, sums = flatten(groups, 3)
    grad = jax.ShapeDtypeStruct((2 * half, width), dtype)
    return pl.pallas_call(
        functools.partial(last_kernel, shape),
        out_shape=[pltpu.VMEM((half, width), jnp.float32)] * 2 + [grad, grad],
        in_specs=[SMEM_SPEC, ANY_SPEC, SMEM_SPEC] + [VMEM_SPEC] * len(args),
        out_specs=[VMEM_SPEC] * 2 + [ANY_SPEC] * 2,
        scratch_shapes=[pltpu.VMEM((2 * half, width), dtype), pltpu.SemaphoreType.DMA((2 * half // PART,))],
        input_output_aliases={sums[1]: 0, sums[2]: 1},
        compiler_params=PARAMS,
        cost_estimate=COST,
    )(scalars, token, parity, *args)


def close_kernel(parity, gy0, gy1, back, _, __, clip_grad, caption_grad, held, sem):
    half = gy0.shape[0]
    waits = []
    for r in range(0, 2 * half, PART):
        rows = slice(r, r + PART)
        part = (gy0 if r < half else gy1)[r % half : r % half + PART, :]
        held[rows, :] = (part + back[rows, :].astype(jnp.float32)).astype(held.dtype)
        waits.append(put(parity[0], clip_grad, caption_grad, held, r, sem))
    for wait in waits:
        wait()


def close(parity, gy0, gy1, back, clip_grad, caption_grad):
    grad = jax.ShapeDtypeStruct(back.shape, back.dtype)
    return pl.pallas_call(
        close_kernel,
        out_shape=[grad, grad],
        in_specs=[SMEM_SPEC] + [VMEM_SPEC] * 3 + [ANY_SPEC, ANY_SPEC],
        out_specs=[ANY_SPEC, ANY_SPEC],
        scratch_shapes=[pltpu.VMEM(back.shape, back.dtype), pltpu.SemaphoreType.DMA((back.shape[0] // PART,))],
        input_output_aliases={4: 0, 5: 1},
        compiler_params=PARAMS,
        cost_estimate=COST,
    )(parity, gy0, gy1, back, clip_grad, caption_grad)


def shards(clips, captions, positive, log_scale, bias):
    rows = clips.shape[0]
    count = lax.axis_size("dp")
    mine = lax.axis_index("dp")
    even = mine % 2 == 0
    parity = (mine % 2).astype(jnp.int32)[None]
    scalars = jnp.concatenate([jnp.exp(log_scale), bias])
    evens = range(0, count, 2)
    odds = range(1, count, 2)

    def move(value, pairs):
        return lax.ppermute(value, "dp", [(i, j % count) for i, j in pairs])

    def swap(value):
        return move(value, [(i, i ^ 1) for i in range(count)])

    apart = [(i, i - 2) for i in evens] + [(i, i + 2) for i in odds]
    home = [(i, i - 1) for i in evens] + [(i, i + 1) for i in odds]

    def caption_ids(owner):
        return (owner % count) * rows + jnp.arange(rows, dtype=jnp.int32)

    half = rows // 2

    def halves(value):
        return [value[:half], value[half:]]

    def pick(first, second):
        return [jnp.where(even, a, b) for a, b in zip(halves(first), halves(second))]

    def each(step, block):
        return [step(part) for part in block]

    y = pick(clips, captions)
    u1 = each(lambda part: move(part, apart), y)
    y, clips, captions = lax.optimization_barrier((y, clips, captions))
    x = jnp.where(even, captions, clips)
    w = swap(x)

    other_pos = swap(positive)
    chip_pos = jnp.stack([other_pos, positive])
    next_even = move(chip_pos, [(i, i - 3) for i in odds])
    next_odd = move(chip_pos, [(i, i - 2) for i in odds])
    w, next_even, next_odd = lax.optimization_barrier((w, next_even, next_odd))
    u2 = move(w, apart)
    next_pos = jnp.where(even, next_even, next_odd)

    x_ids = [jnp.where(even, caption_ids(mine), positive)]
    y_ids = halves(jnp.where(even, positive, caption_ids(mine)))
    w_ids = [jnp.where(even, other_pos, caption_ids(mine - 1))]
    u1_ids = halves(jnp.where(even, next_pos[0], caption_ids(mine - 2)))
    v1_ids = halves(jnp.where(even, caption_ids(mine - 1), next_pos[0]))
    u2_ids = [jnp.where(even, next_pos[1], caption_ids(mine - 3))]
    v2_ids = halves(jnp.where(even, caption_ids(mine - 2), next_pos[1]))

    scalars, u1_ids, v1_ids, u2_ids, v2_ids = lax.optimization_barrier((scalars, u1_ids, v1_ids, u2_ids, v2_ids))

    def group(block, ids, cols, sums=(None, None)):
        pairs = [pair for col, col_ids in cols for pair in zip(col, col_ids)]
        return [(part, part_ids, pairs, total) for part, part_ids, total in zip(block, ids, sums)]

    gx, gy0, gy1, token = band(
        scalars,
        jnp.zeros((8, 128), jnp.float32),
        group([x], x_ids, [(y, y_ids), ([w], w_ids)]) + group(y, y_ids, [([x], x_ids)]),
        [(0, 0), (1, 0), (2, 0)],
        [rows, half, half],
    )

    u1, token = after(u1, token)
    v1 = each(swap, u1)
    gv, gx, gy0, gy1, token = band(
        scalars,
        token,
        group(v1, v1_ids, [(u1, u1_ids)]),
        [(0, 0), (0, half)],
        [rows],
        clips.dtype,
        (gx, gy0, gy1),
    )
    back = move(gv, home)
    gx, gy0, gy1, token = band(
        scalars,
        token,
        group([x], x_ids, [(u1, u1_ids)], [gx]),
        [(0, 0)],
        [rows],
        carried=(gy0, gy1),
    )
    u2, token = after(u2, token)
    v2 = each(swap, halves(u2))
    gy0, gy1, gx, token = band(
        scalars,
        token,
        group(y, y_ids, [(v1, v1_ids)], (gy0, gy1)),
        [(0, 0), (1, 0)],
        [half, half],
        carried=(gx,),
    )
    gy0, gy1, clip_grad, caption_grad = last_pair(
        scalars,
        token,
        parity,
        group([x], x_ids, [([u2], u2_ids)], [gx]) + group(y, y_ids, [(v2, v2_ids)], (gy0, gy1)),
        clips.dtype,
    )
    return tuple(close(parity, gy0, gy1, back, clip_grad, caption_grad))


def solution(mesh):
    in_specs = (P("dp", None), P("dp", None), P("dp"), P(), P())
    out_specs = (P("dp", None), P("dp", None))
    return jax.shard_map(shards, mesh=mesh, in_specs=in_specs, out_specs=out_specs, check_vma=False)
```

```python
import functools

import jax
import jax.numpy as jnp
from jax import lax
from jax.experimental import pallas as pl
from jax.experimental.pallas import tpu as pltpu
from jax.sharding import PartitionSpec as P

PART = 512
LOG2_E = 1.4426950408889634
SMEM_SPEC = pl.BlockSpec(memory_space=pltpu.SMEM)
VMEM_SPEC = pl.BlockSpec(memory_space=pltpu.VMEM)
ANY_SPEC = pl.BlockSpec(memory_space=pl.ANY)
COST = pl.CostEstimate(flops=1, bytes_accessed=1, transcendentals=0)
PARAMS = pltpu.CompilerParams(vmem_limit_bytes=24 * 1024 * 1024)


def upright(ids):
    return jnp.transpose(jnp.broadcast_to(ids, (128, ids.shape[1])))[:, :1]


def accumulate(scalars, groups):
    scale = scalars[0]
    slope = -LOG2_E * scale
    start = -LOG2_E * scalars[1]
    work = [
        (g, r, p)
        for g in range(len(groups))
        for r in range(0, groups[g][0].shape[0], PART)
        for p in range(len(groups[g][2]))
    ]

    def logits(item):
        g, r, p = item
        rows, _, cols, _, _ = groups[g]
        return lax.dot_general(
            rows[r : r + PART, :],
            cols[p][0][...],
            (((1,), (1,)), ((), ())),
            preferred_element_type=jnp.float32,
        )

    ahead = logits(work[0])
    total = None
    for n, (g, r, p) in enumerate(work):
        _, row_ids, cols, summed, store = groups[g]
        now = ahead
        if n + 1 < len(work):
            ahead = logits(work[n + 1])
        hit = upright(row_ids[:, r : r + PART]) == cols[p][1][...]
        power = slope * now + start
        share = pl.reciprocal(1.0 + jnp.exp2(jnp.where(hit, -power, power)), approx=True)
        coef = (jnp.where(hit, -scale, scale) * share).astype(jnp.bfloat16)
        term = jnp.dot(coef, cols[p][0][...], preferred_element_type=jnp.float32)
        if p == 0:
            total = term if summed is None else summed[r : r + PART, :] + term
        else:
            total = total + term
        if p == len(cols) - 1:
            store(r, total)


def store_to(ref, base=0):
    def store(r, value):
        ref[base + r : base + r + PART, :] = value.astype(ref.dtype)

    return store


def unpack(shape, refs):
    groups = []
    for pairs, has_sum in shape:
        rows, row_ids = refs.pop(0), refs.pop(0)
        cols = [(refs.pop(0), refs.pop(0)) for _ in range(pairs)]
        groups.append((rows, row_ids, cols, refs.pop(0) if has_sum else None))
    return groups


def flatten(groups, first):
    shape, args, sums = [], [], []
    for rows, row_ids, cols, summed in groups:
        args += [rows, row_ids[None, :]]
        for col, col_ids in cols:
            args += [col, col_ids[None, :]]
        if summed is not None:
            sums.append(first + len(args))
            args.append(summed)
        shape.append((len(cols), summed is not None))
    return shape, args, sums


def band_kernel(shape, places, carried, scalars, _, *refs):
    refs = list(refs)
    groups = unpack(shape, refs)
    outs = refs[carried:]
    accumulate(scalars, [group + (store_to(outs[n], base),) for group, (n, base) in zip(groups, places)])
    refs[-1][...] = jnp.zeros_like(refs[-1])


def band(scalars, token, groups, places, heights, dtype=jnp.float32, carried=()):
    width = groups[0][0].shape[1]
    shape, args, sums = flatten(groups, 2)
    outs = len(heights)
    aliases = {place: n for n, place in enumerate(dict.fromkeys(sums))}
    aliases |= {2 + len(args) + n: outs + n for n in range(len(carried))}
    return pl.pallas_call(
        functools.partial(band_kernel, shape, places, len(carried)),
        out_shape=[pltpu.VMEM((height, width), dtype) for height in heights]
        + [pltpu.VMEM(value.shape, value.dtype) for value in carried]
        + [jax.ShapeDtypeStruct((8, 128), jnp.float32)],
        in_specs=[SMEM_SPEC, ANY_SPEC] + [VMEM_SPEC] * (len(args) + len(carried)),
        out_specs=[VMEM_SPEC] * (outs + len(carried) + 1),
        input_output_aliases=aliases,
        compiler_params=PARAMS,
        cost_estimate=COST,
    )(scalars, token, *args, *carried)


def after(value, token):
    return lax.optimization_barrier((value, token))


def put(parity, even_target, odd_target, held, r, sem):
    rows = slice(r, r + PART)
    to_even = pltpu.make_async_copy(held.at[rows], even_target.at[rows], sem.at[r // PART])
    to_odd = pltpu.make_async_copy(held.at[rows], odd_target.at[rows], sem.at[r // PART])
    pl.when(parity == 0)(to_even.start)
    pl.when(parity != 0)(to_odd.start)
    return to_even.wait


def last_kernel(shape, scalars, _, parity, *refs):
    refs = list(refs)
    groups = unpack(shape, refs)
    gy0, gy1, clip_grad, caption_grad, held, sem = refs
    waits = []

    def store(r, value):
        held[r : r + PART, :] = value.astype(held.dtype)
        waits.append(put(parity[0], caption_grad, clip_grad, held, r, sem))

    stores = [store, store_to(gy0), store_to(gy1)]
    accumulate(scalars, [group + (one,) for group, one in zip(groups, stores)])
    for wait in waits:
        wait()


def last_pair(scalars, token, parity, groups, dtype):
    rows, width = groups[0][0].shape
    half = rows // 2
    shape, args, sums = flatten(groups, 3)
    grad = jax.ShapeDtypeStruct((2 * half, width), dtype)
    return pl.pallas_call(
        functools.partial(last_kernel, shape),
        out_shape=[pltpu.VMEM((half, width), jnp.float32)] * 2 + [grad, grad],
        in_specs=[SMEM_SPEC, ANY_SPEC, SMEM_SPEC] + [VMEM_SPEC] * len(args),
        out_specs=[VMEM_SPEC] * 2 + [ANY_SPEC] * 2,
        scratch_shapes=[pltpu.VMEM((2 * half, width), dtype), pltpu.SemaphoreType.DMA((2 * half // PART,))],
        input_output_aliases={sums[1]: 0, sums[2]: 1},
        compiler_params=PARAMS,
        cost_estimate=COST,
    )(scalars, token, parity, *args)


def close_kernel(parity, gy0, gy1, back, _, __, clip_grad, caption_grad, held, sem):
    half = gy0.shape[0]
    waits = []
    for r in range(0, 2 * half, PART):
        rows = slice(r, r + PART)
        part = (gy0 if r < half else gy1)[r % half : r % half + PART, :]
        held[rows, :] = (part + back[rows, :].astype(jnp.float32)).astype(held.dtype)
        waits.append(put(parity[0], clip_grad, caption_grad, held, r, sem))
    for wait in waits:
        wait()


def close(parity, gy0, gy1, back, clip_grad, caption_grad):
    grad = jax.ShapeDtypeStruct(back.shape, back.dtype)
    return pl.pallas_call(
        close_kernel,
        out_shape=[grad, grad],
        in_specs=[SMEM_SPEC] + [VMEM_SPEC] * 3 + [ANY_SPEC, ANY_SPEC],
        out_specs=[ANY_SPEC, ANY_SPEC],
        scratch_shapes=[pltpu.VMEM(back.shape, back.dtype), pltpu.SemaphoreType.DMA((back.shape[0] // PART,))],
        input_output_aliases={4: 0, 5: 1},
        compiler_params=PARAMS,
        cost_estimate=COST,
    )(parity, gy0, gy1, back, clip_grad, caption_grad)


def shards(clips, captions, positive, log_scale, bias):
    rows = clips.shape[0]
    count = lax.axis_size("dp")
    mine = lax.axis_index("dp")
    even = mine % 2 == 0
    parity = (mine % 2).astype(jnp.int32)[None]
    scalars = jnp.concatenate([jnp.exp(log_scale), bias])
    evens = range(0, count, 2)
    odds = range(1, count, 2)

    def move(value, pairs):
        return lax.ppermute(value, "dp", [(i, j % count) for i, j in pairs])

    def swap(value):
        return move(value, [(i, i ^ 1) for i in range(count)])

    apart = [(i, i - 2) for i in evens] + [(i, i + 2) for i in odds]
    home = [(i, i - 1) for i in evens] + [(i, i + 1) for i in odds]

    def caption_ids(owner):
        return (owner % count) * rows + jnp.arange(rows, dtype=jnp.int32)

    half = rows // 2

    def halves(value):
        return [value[:half], value[half:]]

    def pick(first, second):
        return [jnp.where(even, a, b) for a, b in zip(halves(first), halves(second))]

    def each(step, block):
        return [step(part) for part in block]

    y = pick(clips, captions)
    u1 = each(lambda part: move(part, apart), y)
    y, clips, captions = lax.optimization_barrier((y, clips, captions))
    x = jnp.where(even, captions, clips)
    w = swap(x)

    other_pos = swap(positive)
    chip_pos = jnp.stack([other_pos, positive])
    next_even = move(chip_pos, [(i, i - 3) for i in odds])
    next_odd = move(chip_pos, [(i, i - 2) for i in odds])
    w, next_even, next_odd = lax.optimization_barrier((w, next_even, next_odd))
    u2 = move(w, apart)
    next_pos = jnp.where(even, next_even, next_odd)

    x_ids = [jnp.where(even, caption_ids(mine), positive)]
    y_ids = halves(jnp.where(even, positive, caption_ids(mine)))
    w_ids = [jnp.where(even, other_pos, caption_ids(mine - 1))]
    u1_ids = halves(jnp.where(even, next_pos[0], caption_ids(mine - 2)))
    v1_ids = halves(jnp.where(even, caption_ids(mine - 1), next_pos[0]))
    u2_ids = [jnp.where(even, next_pos[1], caption_ids(mine - 3))]
    v2_ids = halves(jnp.where(even, caption_ids(mine - 2), next_pos[1]))

    scalars, u1_ids, v1_ids, u2_ids, v2_ids = lax.optimization_barrier((scalars, u1_ids, v1_ids, u2_ids, v2_ids))

    def group(block, ids, cols, sums=(None, None)):
        pairs = [pair for col, col_ids in cols for pair in zip(col, col_ids)]
        return [(part, part_ids, pairs, total) for part, part_ids, total in zip(block, ids, sums)]

    gx, gy0, gy1, token = band(
        scalars,
        jnp.zeros((8, 128), jnp.float32),
        group([x], x_ids, [(y, y_ids), ([w], w_ids)]) + group(y, y_ids, [([x], x_ids)]),
        [(0, 0), (1, 0), (2, 0)],
        [rows, half, half],
    )

    u1, token = after(u1, token)
    v1 = each(swap, u1)
    gv, gx, gy0, gy1, token = band(
        scalars,
        token,
        group(v1, v1_ids, [(u1, u1_ids)]),
        [(0, 0), (0, half)],
        [rows],
        clips.dtype,
        (gx, gy0, gy1),
    )
    back = move(gv, home)
    gx, gy0, gy1, token = band(
        scalars,
        token,
        group([x], x_ids, [(u1, u1_ids)], [gx]),
        [(0, 0)],
        [rows],
        carried=(gy0, gy1),
    )
    u2, token = after(u2, token)
    v2 = each(swap, halves(u2))
    gy0, gy1, gx, token = band(
        scalars,
        token,
        group(y, y_ids, [(v1, v1_ids)], (gy0, gy1)),
        [(0, 0), (1, 0)],
        [half, half],
        carried=(gx,),
    )
    gy0, gy1, clip_grad, caption_grad = last_pair(
        scalars,
        token,
        parity,
        group([x], x_ids, [([u2], u2_ids)], [gx]) + group(y, y_ids, [(v2, v2_ids)], (gy0, gy1)),
        clips.dtype,
    )
    return tuple(close(parity, gy0, gy1, back, clip_grad, caption_grad))


def solution(mesh):
    in_specs = (P("dp", None), P("dp", None), P("dp"), P(), P())
    out_specs = (P("dp", None), P("dp", None))
    return jax.shard_map(shards, mesh=mesh, in_specs=in_specs, out_specs=out_specs, check_vma=False)
```
